32 devices in a mesh: agent: 4 (over y, x), tile: 8 (over z, core).
Axes of the slice: x: 2, y: 2, z: 4, core: 2. Of those that a mesh axis runs over, the one named last changes fastest.
Arguments:
- feats: bfloat16 [32, 32, 24, 256], P('agent', 'tile'), may hold values from -18 to 18
- types: int32 [32], replicated, may hold values from 0 to 1
- valid: int32 [32], replicated, may hold values 0 or 1
- offsets: int32 [32, 2], replicated, may hold values from -2 to 2
- w_qkv: bfloat16 [2, 256, 768], replicated, may hold values from -0.375 to 0.375
- w_out: bfloat16 [2, 256, 256], replicated, may hold values from -0.375 to 0.375
- d_out: bfloat16 [32, 32, 24, 256], P('agent', 'tile'), may hold values from -6 to 6
Outputs:
- d_feats: bfloat16 [32, 32, 24, 256], P('agent', 'tile')
- g_qkv: float32 [2, 256, 768], P(None, 'tile')
- g_out: float32 [2, 256, 256], P(None, 'tile')
The draws below stay inside these ranges and needn't reach their ends.
All inputs are finite; a program needn't handle non-finite values.
Results may differ from the reference program's by a relative error of at most 0.012.
The reference program's roundings to bfloat16 on the way count: a program that leaves them out, or rounds other values in their place, can miss the bound.
Values may be sent and summed in bfloat16 or wider, within the bound.
A program may use at most 128 MiB of HBM per device.

```python
import jax
import jax.numpy as jnp
from jax import lax

C = 256
HEADS = 8
DH = 32
A_DEV = 8
AGENTS = 32
H = 32
GW = 24
MAXOFF = 2


def draw_feats(key, part):
    channel_level = jnp.arange(C, dtype=jnp.float32) / C
    normal_part = jnp.clip(jax.random.normal(key, (AGENTS, H, GW, C), jnp.float32), -6.0, 6.0)
    return (normal_part * 0.3 * jnp.power(10.0, channel_level)).astype(jnp.bfloat16)


def touch_ends(result, key, low, top_value):
    place = [jax.random.randint(jax.random.fold_in(key, axis), (), 0, length) for axis, length in enumerate(result.shape)]
    widest = result.shape.index(max(result.shape))
    next_to = place[:widest] + [(place[widest] + 1) % result.shape[widest]] + place[widest + 1:]
    return result.at[tuple(place)].set(low).at[tuple(next_to)].set(top_value)


def steps_of(own_key, extent, split, smallest, top_value):
    def one(dim, blocks):
        steps = jax.random.uniform(jax.random.fold_in(jax.random.fold_in(own_key, 6), dim), (blocks,), jnp.float32, smallest / len(split), top_value / len(split))
        return jnp.repeat(jnp.exp(steps), extent[dim] // blocks).reshape((-1,) + (1,) * (len(extent) - dim - 1))

    loudness = one(*split[0])
    for cut in split[1:]:
        loudness = loudness * one(*cut)
    return loudness


def normal_values(rng, shape, spread, limit, split=(), kind=jnp.bfloat16):
    gain = steps_of(rng, shape, split, -0.22, 0.18) if split else 1.0
    entries = jax.random.normal(rng, shape, jnp.float32) * spread * gain
    return jnp.minimum(jnp.maximum(entries, -limit), limit).astype(kind)


def setup_inputs(seed: int = 0) -> dict:
    key_list = jax.random.split(jax.random.key(seed), 8)
    feats = draw_feats(jax.random.fold_in(key_list[7], 71), 0)
    types = touch_ends(jax.random.randint(key_list[1], (AGENTS,), 0, 2), jax.random.fold_in(key_list[1], 1), 0, 1).astype(jnp.int32)
    valid = touch_ends((jax.random.randint(key_list[2], (AGENTS,), 0, 4) < 3).astype(jnp.int32), jax.random.fold_in(key_list[2], 1), 0, 1)
    offsets = touch_ends(jax.random.randint(key_list[3], (AGENTS, 2), -MAXOFF, MAXOFF + 1), jax.random.fold_in(key_list[3], 1), -MAXOFF, MAXOFF).astype(jnp.int32)
    w_qkv = normal_values(key_list[4], (2, C, 3 * C), C ** -0.5, 0.375)
    w_out = normal_values(key_list[5], (2, C, C), C ** -0.5, 0.375)
    d_out = normal_values(key_list[6], (AGENTS, H, GW, C), 1.0, 6.0, ((0, 4), (1, 8)))
    return {"feats": feats, "types": types, "valid": valid, "offsets": offsets, "w_qkv": w_qkv, "w_out": w_out, "d_out": d_out}


def relocate(field, offsets, direction):
    padded = jnp.pad(field, ((0, 0), (MAXOFF, MAXOFF), (MAXOFF, MAXOFF), (0, 0)))
    row_count = field.shape[1]
    col_count = field.shape[2]

    def pick_one(plane, offset):
        row_start = (MAXOFF + direction * offset[0]).astype(jnp.int32)
        col_start = (MAXOFF + direction * offset[1]).astype(jnp.int32)
        return lax.dynamic_slice(plane, (row_start, col_start, jnp.int32(0)), (row_count, col_count, plane.shape[2]))
    return jax.vmap(pick_one)(padded, offsets)

def reference(feats, types, valid, offsets, w_qkv, w_out, d_out):
    f32 = jnp.float32
    bf16 = jnp.bfloat16
    groups_n = AGENTS // A_DEV
    score_scale = DH ** (-0.5)
    warped = relocate(feats, offsets, 1)
    wqkv_all = jnp.take(w_qkv, types, axis=0).astype(f32)
    wout_all = jnp.take(w_out, types, axis=0).astype(f32)
    type_hot = (types[:, None] == jnp.arange(2)[None, :]).astype(f32)
    agent_ids = jnp.arange(AGENTS)
    allowed = (valid[None, :] == 1) | (agent_ids[:, None] == agent_ids[None, :])

    def one_row(totals, slices):
        row_feats, row_grads = slices
        feats_wide = row_feats.astype(f32)
        grads_wide = row_grads.astype(f32)
        qkv = jnp.einsum('agc,ace->age', feats_wide, wqkv_all).astype(bf16).astype(f32)
        query = qkv[..., :C].reshape(AGENTS, GW, HEADS, DH)
        keys = qkv[..., C:2 * C].reshape(AGENTS, GW, HEADS, DH)
        values = qkv[..., 2 * C:].reshape(AGENTS, GW, HEADS, DH)
        scores = jnp.einsum('aghd,bghd->ghab', query, keys) * score_scale
        raised = jnp.where(allowed, jnp.exp(scores), f32(0.0))
        attn_prob = raised / lax.optimization_barrier(jnp.sum(raised, axis=-1, keepdims=True))
        prob_low = attn_prob.astype(bf16).astype(f32)
        attended = jnp.einsum('ghab,bghd->aghd', prob_low, values).astype(bf16).astype(f32).reshape(AGENTS, GW, C)
        d_attended = jnp.einsum('age,ace->agc', grads_wide, wout_all).astype(bf16).astype(f32)
        raw_out = jnp.einsum('at,agc,age->tce', type_hot, attended, grads_wide)
        attended_heads = d_attended.reshape(AGENTS, GW, HEADS, DH)
        prob_grad = jnp.einsum('aghd,bghd->ghab', attended_heads, values)
        score_grad = (attn_prob * (prob_grad - lax.optimization_barrier(jnp.sum(attn_prob * prob_grad, axis=-1, keepdims=True))) * score_scale).astype(bf16).astype(f32)
        d_query = jnp.einsum('ghab,bghd->aghd', score_grad, keys).astype(bf16).astype(f32).reshape(AGENTS, GW, C)
        grad_blocks = score_grad.reshape(GW, HEADS, groups_n, A_DEV, AGENTS)
        prob_blocks = prob_low.reshape(GW, HEADS, groups_n, A_DEV, AGENTS)
        query_blocks = query.reshape(groups_n, A_DEV, GW, HEADS, DH)
        dattn_blocks = attended_heads.reshape(groups_n, A_DEV, GW, HEADS, DH)
        key_parts = jnp.einsum('ghnyb,nyghd->nbghd', grad_blocks, query_blocks).astype(bf16).astype(f32)
        value_parts = jnp.einsum('ghnyb,nyghd->nbghd', prob_blocks, dattn_blocks).astype(bf16).astype(f32)
        key_sum = lax.optimization_barrier(jnp.sum(key_parts, axis=0)).reshape(AGENTS, GW, C)
        value_sum = lax.optimization_barrier(jnp.sum(value_parts, axis=0)).reshape(AGENTS, GW, C)
        d_qkv = jnp.concatenate([d_query, key_sum, value_sum], axis=-1)
        d_warped = jnp.einsum('bge,bce->bgc', d_qkv, wqkv_all).astype(bf16)
        raw_qkv = jnp.einsum('bt,bgc,bge->tce', type_hot, feats_wide, d_qkv)
        return ((totals[0] + raw_qkv, totals[1] + raw_out), d_warped)
    start_totals = (jnp.zeros((2, C, 3 * C), f32), jnp.zeros((2, C, C), f32))
    rows_in = (jnp.transpose(warped, (1, 0, 2, 3)), jnp.transpose(d_out, (1, 0, 2, 3)))
    totals, stacked = lax.scan(one_row, start_totals, rows_in)
    d_warped = jnp.transpose(stacked, (1, 0, 2, 3))
    d_feats = relocate(d_warped, offsets, -1)
    raw_qkv, raw_out = totals
    norm_value = jnp.sqrt(jnp.sum(raw_qkv * raw_qkv) + jnp.sum(raw_out * raw_out))
    norm_limit = jnp.sqrt(f32(8.0 * C * C))
    factor = norm_limit / jnp.maximum(norm_value, norm_limit)
    return (d_feats, raw_qkv * factor, raw_out * factor)
```

```python
import functools
import math

import jax
import jax.numpy as jnp
from jax import lax
from jax.experimental import pallas as pl
from jax.experimental.pallas import tpu as pltpu
from jax.sharding import PartitionSpec as P

HEADS = 8
MAXOFF = 2
F32 = jnp.float32
BF16 = jnp.bfloat16


def dot(a, b, ca, cb):
    return lax.dot_general(a, b, (((ca,), (cb,)), ((), ())), preferred_element_type=F32)


def layer_kernel(agents, cells, x_ref, g_ref, types_ref, valid_ref, wqkv_ref, wout_ref, dx_ref, raw_ref,
                 qkv_s, da_s, att_s, dqkv_s, head_s):
    channels = x_ref.shape[1]
    head = channels // HEADS
    scale = head ** (-0.5)
    wide = HEADS * agents
    group = max(1, 256 // agents)
    while cells % group:
        group -= 1
    rows = group * agents
    is_one = types_ref[...] == 1
    type_wide = jnp.broadcast_to(is_one, (agents, channels)).astype(F32)
    type_rows = jnp.concatenate([type_wide] * group, axis=0)
    owner = lax.broadcasted_iota(jnp.int32, (wide, channels), 0) // agents
    lane = lax.broadcasted_iota(jnp.int32, (wide, channels), 1) // head
    head_s[...] = (owner == lane).astype(F32).astype(BF16)

    def project(i, _):
        at = pl.ds(pl.multiple_of(i * rows, rows), rows)
        x = x_ref[at, :]
        g = g_ref[at, :]
        for j in range(3):
            cols = slice(j * channels, (j + 1) * channels)
            a = dot(x, wqkv_ref[0, :, cols], 1, 0)
            b = dot(x, wqkv_ref[1, :, cols], 1, 0)
            qkv_s[at, cols] = jnp.where(type_rows > 0.5, b, a).astype(BF16)
        a = dot(g, wout_ref[0], 1, 1)
        b = dot(g, wout_ref[1], 1, 1)
        da_s[at, :] = jnp.where(type_rows > 0.5, b, a).astype(BF16)
        return 0

    lax.fori_loop(0, cells // group, project, 0)

    key_id = lax.broadcasted_iota(jnp.int32, (agents, wide), 0)
    query_id = lax.broadcasted_iota(jnp.int32, (agents, wide), 1) % agents
    allowed = (jnp.broadcast_to(valid_ref[...], (agents, wide)) == 1) | (key_id == query_id)
    lane_head = lax.broadcasted_iota(jnp.int32, (agents, channels), 1) // head

    def own_heads(full):
        out = full[:agents]
        for h in range(1, HEADS):
            out = jnp.where(lane_head == h, full[h * agents:(h + 1) * agents], out)
        return out

    def attend(i, _):
        at = pl.ds(pl.multiple_of(i * agents, agents), agents)
        q = qkv_s[at, :channels]
        k = qkv_s[at, channels:2 * channels]
        v = qkv_s[at, 2 * channels:]
        da = da_s[at, :]
        mask = head_s[...]
        qx = jnp.concatenate([q] * HEADS, axis=0) * mask
        dax = jnp.concatenate([da] * HEADS, axis=0) * mask
        scores = dot(k, qx, 1, 1) * scale
        raised = jnp.where(allowed, jnp.exp(scores), 0.0)
        prob = raised / jnp.sum(raised, axis=0, keepdims=True)
        low = prob.astype(BF16)
        pg = dot(v, dax, 1, 1)
        sg = (prob * (pg - jnp.sum(prob * pg, axis=0, keepdims=True)) * scale).astype(BF16)
        dqkv_s[at, channels:2 * channels] = dot(sg, qx, 1, 0).astype(BF16)
        dqkv_s[at, 2 * channels:] = dot(low, dax, 1, 0).astype(BF16)
        att_s[at, :] = own_heads(dot(low, v, 0, 0)).astype(BF16)
        dqkv_s[at, :channels] = own_heads(dot(sg, k, 0, 0)).astype(BF16)
        return 0

    lax.fori_loop(0, cells, attend, 0, unroll=4)

    def back(i, _):
        at = pl.ds(pl.multiple_of(i * rows, rows), rows)
        d = dqkv_s[at, :]
        a = dot(d, wqkv_ref[0], 1, 1)
        b = dot(d, wqkv_ref[1], 1, 1)
        dx_ref[at, :] = jnp.where(type_rows > 0.5, b, a).astype(BF16)
        return 0

    lax.fori_loop(0, cells // group, back, 0)

    ones = jnp.concatenate([type_wide.astype(BF16)] * cells, axis=0)
    for t in range(2):
        pick = ones if t else (1 - ones).astype(BF16)
        xt = x_ref[...] * pick
        for j in range(3):
            cols = slice(j * channels, (j + 1) * channels)
            raw_ref[t, :, cols] = dot(xt, dqkv_s[:, cols], 0, 0).astype(BF16)
        raw_ref[t, :, 3 * channels:] = dot(att_s[...] * pick, g_ref[...], 0, 0).astype(BF16)


def layer(x, g, types, valid, w_qkv, w_out):
    cells, agents, channels = x.shape
    n = cells * agents
    vmem = pl.BlockSpec(memory_space=pltpu.VMEM)
    dx, raw = pl.pallas_call(
        functools.partial(layer_kernel, agents, cells),
        out_shape=(
            jax.ShapeDtypeStruct((n, channels), BF16),
            jax.ShapeDtypeStruct((2, channels, 4 * channels), BF16),
        ),
        in_specs=[vmem] * 6,
        out_specs=(vmem, vmem),
        scratch_shapes=[
            pltpu.VMEM((n, 3 * channels), BF16),
            pltpu.VMEM((n, channels), BF16),
            pltpu.VMEM((n, channels), BF16),
            pltpu.VMEM((n, 3 * channels), BF16),
            pltpu.VMEM((HEADS * agents, channels), BF16),
        ],
        compiler_params=pltpu.CompilerParams(vmem_limit_bytes=40 * 2**20),
        cost_estimate=pl.CostEstimate(flops=8 * 10**9, bytes_accessed=5 * 10**6, transcendentals=n * 256),
    )(x.reshape(n, channels), g.reshape(n, channels), types[:, None], valid[:, None], w_qkv, w_out)
    return dx.reshape(cells, agents, channels), raw


def with_halo(cells, width):
    count = lax.axis_size("tile")
    ends = count - 1
    head = cells[:, :width]
    tail = cells[:, cells.shape[1] - width:]
    return jnp.concatenate(
        [
            lax.ppermute(tail, "tile", [(i, i + 1) for i in range(ends)]),
            cells,
            lax.ppermute(head, "tile", [(i + 1, i) for i in range(ends)]),
        ],
        axis=1,
    )


def relocate(rimmed, offsets, direction):
    padded = jnp.pad(rimmed, ((0, 0), (0, 0), (MAXOFF, MAXOFF), (0, 0)))
    row_count = rimmed.shape[1] - 2 * MAXOFF
    col_count = rimmed.shape[2]
    planes = []
    for a in range(rimmed.shape[0]):
        start = (MAXOFF + direction * offsets[a, 0], MAXOFF + direction * offsets[a, 1], jnp.int32(0))
        planes.append(lax.dynamic_slice(padded[a], start, (row_count, col_count, rimmed.shape[3])))
    return planes


def body(feats, types, valid, offsets, w_qkv, w_out, d_out):
    own, row_count, col_count, channels = feats.shape
    parts = lax.axis_size("agent")
    tiles = lax.axis_size("tile")
    local = row_count * col_count
    first = lax.axis_index("agent") * own
    own_offsets = lax.dynamic_slice_in_dim(offsets, first, own, 0)
    grads = jnp.swapaxes(d_out.reshape(own, local, channels), 0, 1)
    all_grads = lax.all_to_all(grads, "agent", split_axis=0, concat_axis=1, tiled=True)
    planes = relocate(with_halo(feats, MAXOFF), own_offsets, 1)
    warped = jnp.stack([p.reshape(local, channels) for p in planes], axis=1)
    all_feats = lax.all_to_all(warped, "agent", split_axis=0, concat_axis=1, tiled=True)
    d_part, raw = layer(all_feats, all_grads, types, valid, w_qkv, w_out)
    returned = lax.all_to_all(d_part, "agent", split_axis=1, concat_axis=0, tiled=True)
    d_warped = jnp.swapaxes(returned, 0, 1).reshape(own, row_count, col_count, channels)
    d_feats = jnp.stack(relocate(with_halo(d_warped, MAXOFF), own_offsets, -1))

    width = raw.shape[2]
    rows = channels // tiles
    chips = tiles // 2
    pairs = [[2 * i, 2 * i + 1] for i in range(chips)]
    lines = [[2 * i + c for i in range(chips)] for c in range(2)]
    part = raw.reshape(2, chips, 2, rows, width).transpose(2, 0, 1, 3, 4)
    part = lax.all_to_all(part, "tile", 0, 0, axis_index_groups=pairs, tiled=True)
    part = jnp.sum(part.astype(F32), axis=0).astype(BF16)
    part = part.reshape(2, chips, rows, parts, width // parts).transpose(3, 1, 0, 2, 4)
    part = lax.all_to_all(part, "agent", 0, 0, tiled=True)
    part = jnp.sum(part.astype(F32), axis=0).astype(BF16)
    part = lax.all_to_all(part, "tile", 0, 0, axis_index_groups=lines, tiled=True)
    part = jnp.sum(part.astype(F32), axis=0)
    squares = jnp.full((8, 128), jnp.sum(part * part), F32)
    total = jnp.sum(lax.all_gather(squares, ("agent", "tile"))[:, 0, 0])
    whole = lax.all_gather(part, "agent")
    limit = math.sqrt(8.0 * channels * channels)
    factor = limit / jnp.maximum(jnp.sqrt(total), limit)
    whole = whole.transpose(1, 2, 0, 3).reshape(2, rows, width) * factor
    return (d_feats, whole[..., :3 * channels], whole[..., 3 * channels:])


def solution(mesh):
    placed = (
        P("agent", "tile", None, None),
        P(),
        P(),
        P(),
        P(),
        P(),
        P("agent", "tile", None, None),
    )
    return jax.shard_map(
        body,
        mesh=mesh,
        in_specs=placed,
        out_specs=(P("agent", "tile", None, None), P(None, "tile", None), P(None, "tile", None)),
        check_vma=False,
    )
```

```python
import functools
import math

import jax
import jax.numpy as jnp
from jax import lax
from jax.experimental import pallas as pl
from jax.experimental.pallas import tpu as pltpu
from jax.sharding import PartitionSpec as P

HEADS = 8
MAXOFF = 2
F32 = jnp.float32
BF16 = jnp.bfloat16


def dot(a, b, ca, cb):
    return lax.dot_general(a, b, (((ca,), (cb,)), ((), ())), preferred_element_type=F32)


def layer_kernel(agents, cells, own, tiles, x_ref, g_ref, types_ref, valid_ref, wqkv_ref, wout_ref, dx_ref, raw_ref,
                 qkv_s, da_s, att_s, dqkv_s, head_s):
    channels = x_ref.shape[1]
    head = channels // HEADS
    scale = head ** (-0.5)
    wide = HEADS * agents
    group = max(1, 256 // agents)
    while cells % group:
        group -= 1
    rows = group * agents
    is_one = types_ref[...] == 1
    type_wide = jnp.broadcast_to(is_one, (agents, channels)).astype(F32)
    type_rows = jnp.concatenate([type_wide] * group, axis=0)
    owner = lax.broadcasted_iota(jnp.int32, (wide, channels), 0) // agents
    lane = lax.broadcasted_iota(jnp.int32, (wide, channels), 1) // head
    head_s[...] = (owner == lane).astype(F32).astype(BF16)

    def project(i, _):
        at = pl.ds(pl.multiple_of(i * rows, rows), rows)
        x = x_ref[at, :]
        g = g_ref[at, :]
        for j in range(3):
            cols = slice(j * channels, (j + 1) * channels)
            a = dot(x, wqkv_ref[0, :, cols], 1, 0)
            b = dot(x, wqkv_ref[1, :, cols], 1, 0)
            qkv_s[at, cols] = jnp.where(type_rows > 0.5, b, a).astype(BF16)
        a = dot(g, wout_ref[0], 1, 1)
        b = dot(g, wout_ref[1], 1, 1)
        da_s[at, :] = jnp.where(type_rows > 0.5, b, a).astype(BF16)
        return 0

    lax.fori_loop(0, cells // group, project, 0)

    key_id = lax.broadcasted_iota(jnp.int32, (agents, wide), 0)
    query_id = lax.broadcasted_iota(jnp.int32, (agents, wide), 1) % agents
    allowed = (jnp.broadcast_to(valid_ref[...], (agents, wide)) == 1) | (key_id == query_id)
    lane_head = lax.broadcasted_iota(jnp.int32, (agents, channels), 1) // head

    def own_heads(full):
        out = full[:agents]
        for h in range(1, HEADS):
            out = jnp.where(lane_head == h, full[h * agents:(h + 1) * agents], out)
        return out

    def attend(i, _):
        at = pl.ds(pl.multiple_of(i * agents, agents), agents)
        q = qkv_s[at, :channels]
        k = qkv_s[at, channels:2 * channels]
        v = qkv_s[at, 2 * channels:]
        da = da_s[at, :]
        mask = head_s[...]
        qx = jnp.concatenate([q] * HEADS, axis=0) * mask
        dax = jnp.concatenate([da] * HEADS, axis=0) * mask
        scores = dot(k, qx, 1, 1) * scale
        raised = jnp.where(allowed, jnp.exp(scores), 0.0)
        prob = raised / jnp.sum(raised, axis=0, keepdims=True)
        low = prob.astype(BF16)
        pg = dot(v, dax, 1, 1)
        sg = (prob * (pg - jnp.sum(prob * pg, axis=0, keepdims=True)) * scale).astype(BF16)
        dqkv_s[at, channels:2 * channels] = dot(sg, qx, 1, 0).astype(BF16)
        dqkv_s[at, 2 * channels:] = dot(low, dax, 1, 0).astype(BF16)
        att_s[at, :] = own_heads(dot(low, v, 0, 0)).astype(BF16)
        dqkv_s[at, :channels] = own_heads(dot(sg, k, 0, 0)).astype(BF16)
        return 0

    lax.fori_loop(0, cells, attend, 0, unroll=4)

    def back(i, _):
        at = pl.ds(pl.multiple_of(i * rows, rows), rows)
        d = dqkv_s[at, :]
        a = dot(d, wqkv_ref[0], 1, 1)
        b = dot(d, wqkv_ref[1], 1, 1)
        full = jnp.where(type_rows > 0.5, b, a).reshape(group, agents, channels)
        for n in range(agents // own):
            part = full[:, n * own:(n + 1) * own].reshape(group * own, channels)
            dx_ref[n, pl.ds(pl.multiple_of(i * group * own, group * own), group * own), :] = part.astype(BF16)
        return 0

    lax.fori_loop(0, cells // group, back, 0)

    ones = jnp.concatenate([type_wide.astype(BF16)] * cells, axis=0)
    share = channels // tiles
    for t in range(2):
        pick = ones if t else (1 - ones).astype(BF16)
        xt = x_ref[...] * pick
        for j in range(4):
            if j < 3:
                full = dot(xt, dqkv_s[:, j * channels:(j + 1) * channels], 0, 0)
            else:
                full = dot(att_s[...] * pick, g_ref[...], 0, 0)
            for i in range(tiles):
                raw_ref[i % 2, j, i // 2, t * share:(t + 1) * share, :] = full[i * share:(i + 1) * share].astype(BF16)


VMEM = pl.BlockSpec(memory_space=pltpu.VMEM)
MESH = pl.DeviceIdType.MESH


def layer(x, g, types, valid, w_qkv, w_out, own, tiles):
    n, channels = x.shape
    agents = types.shape[0]
    cells = n // agents
    parts = agents // own
    return pl.pallas_call(
        functools.partial(layer_kernel, agents, cells, own, tiles),
        out_shape=(
            jax.ShapeDtypeStruct((parts, cells * own, channels), BF16),
            jax.ShapeDtypeStruct((2, 4, tiles // 2, 2 * channels // tiles, channels), BF16),
        ),
        in_specs=[VMEM] * 6,
        out_specs=(VMEM, VMEM),
        scratch_shapes=[
            pltpu.VMEM((n, 3 * channels), BF16),
            pltpu.VMEM((n, channels), BF16),
            pltpu.VMEM((n, channels), BF16),
            pltpu.VMEM((n, 3 * channels), BF16),
            pltpu.VMEM((HEADS * agents, channels), BF16),
        ],
        compiler_params=pltpu.CompilerParams(vmem_limit_bytes=40 * 2**20),
        cost_estimate=pl.CostEstimate(flops=8 * 10**9, bytes_accessed=5 * 10**6, transcendentals=n * 256),
    )(x, g, types[:, None], valid[:, None], w_qkv, w_out)


def one_hot(target, width):
    lanes = lax.broadcasted_iota(jnp.int32, (target.shape[0], width), 1)
    return jnp.where(lanes == target, 1.0, 0.0).astype(BF16)


def greet(others):
    barrier = pltpu.get_barrier_semaphore()
    for there, device in others:
        @pl.when(there)
        def _(device=device):
            pl.semaphore_signal(barrier, inc=1, device_id=device, device_id_type=MESH)
    count = sum(jnp.where(there, 1, 0) for there, _ in others)
    pl.semaphore_wait(barrier, count)


def sender(src, dst, sems, k, device):
    return pltpu.make_async_remote_copy(
        src_ref=src, dst_ref=dst, send_sem=sems.at[0, k], recv_sem=sems.at[1, k], device_id=device, device_id_type=MESH
    )


def front_kernel(parts, tiles, feats_ref, grads_ref, warp_ref, turn_ref, x_ref, g_ref,
                 rim, x_send, g_send, x_recv, g_recv, halo_sem, x_sem, g_sem):
    me, tile = lax.axis_index("agent"), lax.axis_index("tile")
    own, local, channels = feats_ref.shape
    cells = local // parts
    edge = MAXOFF * cells
    inner = rim.shape[1]
    left, right = tile > 0, tile < tiles - 1
    peers = [lax.rem(me + k, parts) for k in range(parts)]
    greet([(left, (me, tile - 1)), (right, (me, tile + 1))] + [(parts > 0, (peers[k], tile)) for k in range(1, parts)])
    to_right = sender(feats_ref.at[:, local - edge:, :], rim.at[:, :edge, :], halo_sem, 0, (me, tile + 1))
    to_left = sender(feats_ref.at[:, :edge, :], rim.at[:, inner - edge:, :], halo_sem, 1, (me, tile - 1))

    @pl.when(right)
    def _():
        to_right.start()

    @pl.when(left)
    def _():
        to_left.start()

    @pl.when(tile == 0)
    def _():
        rim[:, :edge, :] = jnp.zeros((own, edge, channels), BF16)

    @pl.when(tile == tiles - 1)
    def _():
        rim[:, inner - edge:, :] = jnp.zeros((own, edge, channels), BF16)

    rim[:, edge:inner - edge, :] = feats_ref[...]

    def spread(source, target, send, recv, sems):
        copies = []
        for k in (*range(1, parts), 0):
            pick = one_hot(target + peers[k] * cells, source.shape[0])
            value = dot(pick, source, 1, 0).astype(BF16)
            if k == 0:
                recv[me] = value
            else:
                send[k] = value
                copies.append(sender(send.at[k], recv.at[me], sems, k, (peers[k], tile)))
                copies[-1].start()
        return copies

    def gather(copies, recv, out):
        for copy in copies:
            copy.wait()
        pieces = [recv[n].astype(F32).reshape(cells, own, channels) for n in range(parts)]
        out[...] = jnp.concatenate(pieces, axis=1).reshape(cells * own * parts, channels).astype(BF16)

    g_copies = spread(grads_ref[...].reshape(own * local, channels), turn_ref[...], g_send, g_recv, g_sem)

    @pl.when(left)
    def _():
        to_right.wait_recv()
        to_left.wait_send()

    @pl.when(right)
    def _():
        to_left.wait_recv()
        to_right.wait_send()

    x_copies = spread(rim[...].reshape(own * inner, channels), warp_ref[...], x_send, x_recv, x_sem)
    gather(g_copies, g_recv, g_ref)
    gather(x_copies, x_recv, x_ref)


def front(feats, grads, warp, turn, parts, tiles):
    own, local, channels = feats.shape
    cells = local // parts
    inner = local + 2 * MAXOFF * cells
    out = jax.ShapeDtypeStruct((own * local, channels), BF16)
    block = pltpu.VMEM((parts, cells * own, channels), BF16)
    return pl.pallas_call(
        functools.partial(front_kernel, parts, tiles),
        out_shape=(out, out),
        in_specs=[VMEM] * 4,
        out_specs=(VMEM, VMEM),
        scratch_shapes=[
            pltpu.VMEM((own, inner, channels), BF16),
            block, block, block, block,
            pltpu.SemaphoreType.DMA((2, 2)),
            pltpu.SemaphoreType.DMA((2, parts)),
            pltpu.SemaphoreType.DMA((2, parts)),
        ],
        compiler_params=pltpu.CompilerParams(
            collective_id=0, has_side_effects=True, vmem_limit_bytes=40 * 2**20
        ),
    )(feats, grads, warp, turn)


def back_kernel(parts, tiles, dx_ref, raw_ref, turn_ref, df_ref, gq_ref, go_ref,
                rim, pair, first, agent_in, second, line_in, final, every, square, squares,
                dx_sem, halo_sem, pair_sem, agent_sem, line_sem, every_sem, square_sem):
    me, tile = lax.axis_index("agent"), lax.axis_index("tile")
    core, chip = lax.rem(tile, 2), tile // 2
    chips = tiles // 2
    channels = dx_ref.shape[2]
    share = channels // tiles
    left, right = tile > 0, tile < tiles - 1
    peers = [lax.rem(me + k, parts) for k in range(parts)]
    always = parts > 0
    greet(
        [(always, (peers[k], tile)) for k in range(1, parts)]
        + [(always, (me, lax.rem(tile + k, tiles))) for k in range(1, tiles)]
        + [(left, (peers[k], tile - 1)) for k in range(1, parts)]
        + [(right, (peers[k], tile + 1)) for k in range(1, parts)]
    )
    swap = sender(raw_ref.at[1 - core], pair, pair_sem, 0, (me, tile + 1 - 2 * core))
    swap.start()
    low = me < MAXOFF
    next_tile = jnp.where(low, tile - 1, tile + 1)
    next_row = jnp.where(low, me + parts + MAXOFF, me - (parts - MAXOFF))
    there = (next_tile >= 0) & (next_tile < tiles)
    homes = [sender(dx_ref.at[peers[k]], rim.at[me + MAXOFF], dx_sem, k, (peers[k], tile)) for k in range(1, parts)]
    for copy in homes:
        copy.start()
    sides = [sender(dx_ref.at[peers[k]], rim.at[next_row], halo_sem, k, (peers[k], next_tile)) for k in range(parts)]

    @pl.when(there)
    def _():
        for copy in sides:
            copy.start()

    rows = dx_ref.shape[1]

    @pl.when(tile == 0)
    def _():
        rim[:MAXOFF] = jnp.zeros((MAXOFF, rows, channels), BF16)

    @pl.when(tile == tiles - 1)
    def _():
        rim[parts + MAXOFF:] = jnp.zeros((MAXOFF, rows, channels), BF16)

    rim[me + MAXOFF] = dx_ref[me]
    swap.wait()
    first[...] = (raw_ref[core].astype(F32) + pair[...].astype(F32)).astype(BF16)
    agent_copies = [sender(first.at[peers[k]], agent_in.at[k], agent_sem, k, (peers[k], tile)) for k in range(1, parts)]
    for copy in agent_copies:
        copy.start()
    for copy in agent_copies:
        copy.wait()
    total = first[me].astype(F32)
    for k in range(1, parts):
        total = total + agent_in[k].astype(F32)
    second[...] = total.astype(BF16)
    line_copies = []
    for k in range(1, chips):
        other = lax.rem(chip + k, chips)
        line_copies.append(sender(second.at[other], line_in.at[k], line_sem, k, (me, 2 * other + core)))
        line_copies[-1].start()

    for copy in homes:
        copy.wait()
    for k in range(parts):
        origin = lax.rem(me + parts - k, parts)
        arrives = jnp.where(origin < MAXOFF, tile + 1, tile - 1)

        @pl.when((arrives >= 0) & (arrives < tiles))
        def _(k=k):
            sides[k].wait_recv()

        @pl.when(there)
        def _(k=k):
            sides[k].wait_send()

    source = rim[...].reshape(rim.shape[0] * rows, channels)
    own, local = df_ref.shape[:2]
    for i in range(0, own, 2):
        pick = one_hot(turn_ref[i * local:(i + 2) * local, :], source.shape[0])
        df_ref[i:i + 2] = dot(pick, source, 1, 0).reshape(2, local, channels).astype(BF16)

    for copy in line_copies:
        copy.wait()
    total = second[chip].astype(F32)
    for k in range(1, chips):
        total = total + line_in[k].astype(F32)
    final[...] = total.astype(BF16)
    every[me] = total.astype(BF16)
    every_copies = [sender(final, every.at[me], every_sem, k, (peers[k], tile)) for k in range(1, parts)]
    for copy in every_copies:
        copy.start()
    for copy in every_copies:
        copy.wait()
    whole = every[...].astype(F32)
    summed = jnp.sum(whole * whole, axis=0)
    summed = jnp.sum(jnp.sum(summed, axis=0, keepdims=True), axis=1, keepdims=True)
    spread = jnp.broadcast_to(summed, (8, 128))
    square[...] = spread
    squares[tile] = spread
    square_copies = [
        sender(square, squares.at[tile], square_sem, k, (me, lax.rem(tile + k, tiles))) for k in range(1, tiles)
    ]
    for copy in square_copies:
        copy.start()
    for copy in square_copies:
        copy.wait()
    norm = jnp.sqrt(jnp.sum(squares[...], axis=0)[:1, :1])
    limit = math.sqrt(8.0 * channels * channels)
    factor = limit / jnp.maximum(norm, limit)
    for t in range(2):
        for j in range(4):
            piece = every[j].astype(F32)[t * share:(t + 1) * share] * factor
            if j < 3:
                gq_ref[t, :, j * channels:(j + 1) * channels] = piece
            else:
                go_ref[t] = piece


def back(dx, raw, turn, own, tiles):
    parts, rows, channels = dx.shape
    local = parts * rows // own
    share = channels // tiles
    chips = tiles // 2
    dma = lambda n: pltpu.SemaphoreType.DMA((2, n))
    return pl.pallas_call(
        functools.partial(back_kernel, parts, tiles),
        out_shape=(
            jax.ShapeDtypeStruct((own, local, channels), BF16),
            jax.ShapeDtypeStruct((2, share, 3 * channels), F32),
            jax.ShapeDtypeStruct((2, share, channels), F32),
        ),
        in_specs=[VMEM] * 3,
        out_specs=(VMEM,) * 3,
        scratch_shapes=[
            pltpu.VMEM((parts + 2 * MAXOFF, rows, channels), BF16),
            pltpu.VMEM((4, chips, 2 * share, channels), BF16),
            pltpu.VMEM((4, chips, 2 * share, channels), BF16),
            pltpu.VMEM((parts, chips, 2 * share, channels), BF16),
            pltpu.VMEM((chips, 2 * share, channels), BF16),
            pltpu.VMEM((chips, 2 * share, channels), BF16),
            pltpu.VMEM((2 * share, channels), BF16),
            pltpu.VMEM((parts, 2 * share, channels), BF16),
            pltpu.VMEM((8, 128), F32),
            pltpu.VMEM((tiles, 8, 128), F32),
            dma(parts), dma(parts), dma(1), dma(parts), dma(chips), dma(parts), dma(tiles),
        ],
        compiler_params=pltpu.CompilerParams(
            collective_id=1, has_side_effects=True, vmem_limit_bytes=40 * 2**20
        ),
    )(dx, raw, turn)


def body(feats, types, valid, offsets, w_qkv, w_out, d_out):
    own, row_count, col_count, channels = feats.shape
    parts = lax.axis_size("agent")
    tiles = lax.axis_size("tile")
    assert row_count == parts == 4
    local = row_count * col_count
    offs = lax.dynamic_slice_in_dim(offsets, lax.axis_index("agent") * own, own, 0)
    gone = -(1 << 20)
    rows_in = row_count + 2 * MAXOFF
    col = jnp.arange(col_count)[:, None]
    agent = jnp.arange(own)[None, :]
    from_col = col + offs[None, :, 1]
    warp = agent * (rows_in * col_count) + (MAXOFF + offs[None, :, 0]) * col_count + from_col
    warp = jnp.where((from_col >= 0) & (from_col < col_count), warp, gone).reshape(-1, 1).astype(jnp.int32)
    turn = (agent * local + col).reshape(-1, 1).astype(jnp.int32)
    x, g = front(
        feats.reshape(own, local, channels), d_out.reshape(own, local, channels), warp, turn, parts, tiles
    )
    dx, raw = layer(x, g, types, valid, w_qkv, w_out, own, tiles)
    agent = jnp.arange(own)[:, None, None]
    to_row = jnp.arange(row_count)[None, :, None] + MAXOFF - offs[:, 0][:, None, None]
    to_col = jnp.arange(col_count)[None, None, :] - offs[:, 1][:, None, None]
    home = to_row * (col_count * own) + to_col * own + agent
    home = jnp.where((to_col >= 0) & (to_col < col_count), home, gone).reshape(-1, 1).astype(jnp.int32)
    d_feats, g_qkv, g_out = back(dx, raw, home, own, tiles)
    return (d_feats.reshape(feats.shape), g_qkv, g_out)


def solution(mesh):
    placed = (
        P("agent", "tile", None, None),
        P(),
        P(),
        P(),
        P(),
        P(),
        P("agent", "tile", None, None),
    )
    return jax.shard_map(
        body,
        mesh=mesh,
        in_specs=placed,
        out_specs=(P("agent", "tile", None, None), P(None, "tile", None), P(None, "tile", None)),
        check_vma=False,
    )
```

```python
import functools
import math

import jax
import jax.numpy as jnp
from jax import lax
from jax.experimental import pallas as pl
from jax.experimental.pallas import tpu as pltpu
from jax.sharding import PartitionSpec as P

HEADS = 8
MAXOFF = 2
F32 = jnp.float32
BF16 = jnp.bfloat16


def dot(a, b, ca, cb):
    return lax.dot_general(a, b, (((ca,), (cb,)), ((), ())), preferred_element_type=F32)


VMEM = pl.BlockSpec(memory_space=pltpu.VMEM)
HBM = pl.BlockSpec(memory_space=pltpu.HBM)
SMEM = pl.BlockSpec(memory_space=pltpu.SMEM)
MESH = pl.DeviceIdType.MESH
GONE = -(1 << 20)


def one_hot(target, width):
    lanes = lax.broadcasted_iota(jnp.int32, (target.shape[0], width), 1)
    return jnp.where(lanes == target, 1.0, 0.0).astype(BF16)


def greet(others):
    barrier = pltpu.get_barrier_semaphore()
    for there, device in others:
        @pl.when(there)
        def _(device=device):
            pl.semaphore_signal(barrier, inc=1, device_id=device, device_id_type=MESH)
    count = sum(jnp.where(there, 1, 0) for there, _ in others)
    pl.semaphore_wait(barrier, count)


def sender(src, dst, sems, k, device):
    return pltpu.make_async_remote_copy(
        src_ref=src, dst_ref=dst, send_sem=sems.at[0, k], recv_sem=sems.at[1, k], device_id=device, device_id_type=MESH
    )


def spelled(index, values):
    out = jnp.zeros_like(index)
    for j, value in enumerate(values):
        out = jnp.where(index == j, value, out)
    return out


def kernel(parts, tiles, agents, feats_ref, types_ref, valid_ref, offs_ref, wqkv_hbm, wout_hbm, grads_hbm,
           df_ref, gq_ref, go_ref,
           rim, grads, wqkv_ref, wout_ref, x_send, g_send, x_recv, g_recv, x_ref, g_ref,
           qkv_s, da_s, att_s, dqkv_s, head_s, dx, raw, back_rim, pair, first, agent_in, second, line_in,
           final, every, square, squares,
           load_sem, halo_sem, x_sem, g_sem, dx_sem, side_sem, pair_sem, agent_sem, line_sem, every_sem, square_sem):
    me, tile = lax.axis_index("agent"), lax.axis_index("tile")
    core, chip = lax.rem(tile, 2), tile // 2
    chips = tiles // 2
    own, local, channels = feats_ref.shape
    cells = local // parts
    edge = MAXOFF * cells
    inner = rim.shape[1]
    left, right = tile > 0, tile < tiles - 1
    always = parts > 0
    peers = [lax.rem(me + k, parts) for k in range(parts)]

    loads = [
        pltpu.make_async_copy(grads_hbm, grads, load_sem.at[0]),
        pltpu.make_async_copy(feats_ref, rim.at[:, edge:inner - edge, :], load_sem.at[1]),
        pltpu.make_async_copy(wout_hbm, wout_ref, load_sem.at[2]),
        pltpu.make_async_copy(wqkv_hbm, wqkv_ref, load_sem.at[3]),
    ]
    for copy in loads:
        copy.start()
    greet(
        [(always, (peers[k], tile)) for k in range(1, parts)]
        + [(always, (me, lax.rem(tile + k, tiles))) for k in range(1, tiles)]
    )
    to_right = sender(feats_ref.at[:, local - edge:, :], rim.at[:, :edge, :], halo_sem, 0, (me, tile + 1))
    to_left = sender(feats_ref.at[:, :edge, :], rim.at[:, inner - edge:, :], halo_sem, 1, (me, tile - 1))

    @pl.when(right)
    def _():
        to_right.start()

    @pl.when(left)
    def _():
        to_left.start()

    rows = cells * own

    @pl.when(tile == 0)
    def _():
        rim[:, :edge, :] = jnp.zeros((own, edge, channels), BF16)
        back_rim[:MAXOFF] = jnp.zeros((MAXOFF, rows, channels), BF16)

    @pl.when(tile == tiles - 1)
    def _():
        rim[:, inner - edge:, :] = jnp.zeros((own, edge, channels), BF16)
        back_rim[parts + MAXOFF:] = jnp.zeros((MAXOFF, rows, channels), BF16)

    def spread(source, target, send, recv, sems):
        copies = []
        for k in (*range(1, parts), 0):
            pick = one_hot(target + peers[k] * cells, source.shape[0])
            value = dot(pick, source, 1, 0).astype(BF16)
            if k == 0:
                recv[me] = value
            else:
                send[k] = value
                copies.append(sender(send.at[k], recv.at[me], sems, k, (peers[k], tile)))
                copies[-1].start()
        return copies

    def gather(copies, recv, out):
        for copy in copies:
            copy.wait()
        pieces = [recv[n].astype(F32).reshape(cells, own, channels) for n in range(parts)]
        out[...] = jnp.concatenate(pieces, axis=1).reshape(rows * parts, channels).astype(BF16)

    place = lax.broadcasted_iota(jnp.int32, (rows, 1), 0)
    whose, cell = place % own, place // own
    row_off = [offs_ref[me * own + j, 0] for j in range(own)]
    col_off = [offs_ref[me * own + j, 1] for j in range(own)]
    from_col = cell + spelled(whose, col_off)
    warp = whose * inner + (MAXOFF + spelled(whose, row_off)) * cells + from_col
    warp = jnp.where((from_col >= 0) & (from_col < cells), warp, GONE)

    loads[0].wait()
    g_copies = spread(grads[...].reshape(own * local, channels), whose * local + cell, g_send, g_recv, g_sem)
    loads[1].wait()

    @pl.when(left)
    def _():
        to_right.wait_recv()
        to_left.wait_send()

    @pl.when(right)
    def _():
        to_left.wait_recv()
        to_right.wait_send()

    x_copies = spread(rim[...].reshape(own * inner, channels), warp, x_send, x_recv, x_sem)

    size = channels // HEADS
    scale = size ** (-0.5)
    wide = HEADS * agents
    group = 8
    span = group * agents
    agent_col = lax.broadcasted_iota(jnp.int32, (agents, 1), 0)
    kind = spelled(agent_col, [types_ref[j] for j in range(agents)])
    valid = spelled(agent_col, [valid_ref[j] for j in range(agents)])
    type_wide = jnp.broadcast_to(kind, (agents, channels)).astype(F32)
    type_rows = jnp.concatenate([type_wide] * group, axis=0)
    owner = lax.broadcasted_iota(jnp.int32, (wide, channels), 0) // agents
    lane = lax.broadcasted_iota(jnp.int32, (wide, channels), 1) // size
    head_s[...] = jnp.where(owner == lane, 1.0, 0.0).astype(BF16)

    loads[2].wait()
    loads[3].wait()
    gather(g_copies, g_recv, g_ref)

    def project_g(i, _):
        at = pl.ds(pl.multiple_of(i * span, span), span)
        g = g_ref[at, :]
        a = dot(g, wout_ref[0], 1, 1)
        b = dot(g, wout_ref[1], 1, 1)
        da_s[at, :] = jnp.where(type_rows > 0.5, b, a).astype(BF16)
        return 0

    lax.fori_loop(0, cells // group, project_g, 0)
    gather(x_copies, x_recv, x_ref)

    def project(i, _):
        at = pl.ds(pl.multiple_of(i * span, span), span)
        x = x_ref[at, :]
        for j in range(3):
            cols = slice(j * channels, (j + 1) * channels)
            a = dot(x, wqkv_ref[0, :, cols], 1, 0)
            b = dot(x, wqkv_ref[1, :, cols], 1, 0)
            qkv_s[at, cols] = jnp.where(type_rows > 0.5, b, a).astype(BF16)
        return 0

    lax.fori_loop(0, cells // group, project, 0)

    key_id = lax.broadcasted_iota(jnp.int32, (agents, wide), 0)
    query_id = lax.broadcasted_iota(jnp.int32, (agents, wide), 1) % agents
    allowed = (jnp.broadcast_to(valid, (agents, wide)) == 1) | (key_id == query_id)
    lane_head = lax.broadcasted_iota(jnp.int32, (agents, channels), 1) // size

    def own_heads(full):
        out = full[:agents]
        for h in range(1, HEADS):
            out = jnp.where(lane_head == h, full[h * agents:(h + 1) * agents], out)
        return out

    def attend(i, _):
        at = pl.ds(pl.multiple_of(i * agents, agents), agents)
        q = qkv_s[at, :channels]
        k = qkv_s[at, channels:2 * channels]
        v = qkv_s[at, 2 * channels:]
        da = da_s[at, :]
        mask = head_s[...]
        qx = jnp.concatenate([q] * HEADS, axis=0) * mask
        dax = jnp.concatenate([da] * HEADS, axis=0) * mask
        scores = dot(k, qx, 1, 1) * scale
        raised = jnp.where(allowed, jnp.exp(scores), 0.0)
        prob = raised / jnp.sum(raised, axis=0, keepdims=True)
        low = prob.astype(BF16)
        pg = dot(v, dax, 1, 1)
        sg = (prob * (pg - jnp.sum(prob * pg, axis=0, keepdims=True)) * scale).astype(BF16)
        dqkv_s[at, channels:2 * channels] = dot(sg, qx, 1, 0).astype(BF16)
        dqkv_s[at, 2 * channels:] = dot(low, dax, 1, 0).astype(BF16)
        att_s[at, :] = own_heads(dot(low, v, 0, 0)).astype(BF16)
        dqkv_s[at, :channels] = own_heads(dot(sg, k, 0, 0)).astype(BF16)
        return 0

    lax.fori_loop(0, cells, attend, 0, unroll=4)

    share = channels // tiles
    ones = jnp.concatenate([type_wide.astype(BF16)] * cells, axis=0)
    for t in range(2):
        pick = ones if t else (1 - ones).astype(BF16)
        xt = x_ref[...] * pick
        for j in range(4):
            if j < 3:
                full = dot(xt, dqkv_s[:, j * channels:(j + 1) * channels], 0, 0)
            else:
                full = dot(att_s[...] * pick, g_ref[...], 0, 0)
            for i in range(tiles):
                raw[i % 2, j, i // 2, t * share:(t + 1) * share, :] = full[i * share:(i + 1) * share].astype(BF16)
    swap = sender(raw.at[1 - core], pair, pair_sem, 0, (me, tile + 1 - 2 * core))
    swap.start()

    def back(i, _):
        at = pl.ds(pl.multiple_of(i * span, span), span)
        d = dqkv_s[at, :]
        a = dot(d, wqkv_ref[0], 1, 1)
        b = dot(d, wqkv_ref[1], 1, 1)
        full = jnp.where(type_rows > 0.5, b, a).reshape(group, agents, channels)
        for n in range(parts):
            part = full[:, n * own:(n + 1) * own].reshape(group * own, channels)
            dx[n, pl.ds(pl.multiple_of(i * group * own, group * own), group * own), :] = part.astype(BF16)
        return 0

    lax.fori_loop(0, cells // group, back, 0)
    homes = [sender(dx.at[peers[k]], back_rim.at[me + MAXOFF], dx_sem, k, (peers[k], tile)) for k in range(1, parts)]
    for copy in homes:
        copy.start()
    back_rim[me + MAXOFF] = dx[me]

    swap.wait()
    first[...] = (raw[core].astype(F32) + pair[...].astype(F32)).astype(BF16)
    agent_copies = [sender(first.at[peers[k]], agent_in.at[k], agent_sem, k, (peers[k], tile)) for k in range(1, parts)]
    for copy in agent_copies:
        copy.start()

    for copy in homes:
        copy.wait()
    side_left = sender(
        back_rim.at[MAXOFF:2 * MAXOFF], back_rim.at[parts + MAXOFF:], side_sem, 0, (me, tile - 1)
    )
    side_right = sender(back_rim.at[parts:parts + MAXOFF], back_rim.at[:MAXOFF], side_sem, 1, (me, tile + 1))

    @pl.when(left)
    def _():
        side_left.start()

    @pl.when(right)
    def _():
        side_right.start()

    for copy in agent_copies:
        copy.wait()
    total = first[me].astype(F32)
    for k in range(1, parts):
        total = total + agent_in[k].astype(F32)
    second[...] = total.astype(BF16)
    line_copies = []
    for k in range(1, chips):
        other = lax.rem(chip + k, chips)
        line_copies.append(sender(second.at[other], line_in.at[k], line_sem, k, (me, 2 * other + core)))
        line_copies[-1].start()

    @pl.when(left)
    def _():
        side_right.wait_recv()
        side_left.wait_send()

    @pl.when(right)
    def _():
        side_left.wait_recv()
        side_right.wait_send()

    def restore(agent_ids):
        source = back_rim[...].reshape(back_rim.shape[0] * rows, channels)
        spot = lax.broadcasted_iota(jnp.int32, (local, 1), 0)
        for i in agent_ids:
            col = spot % cells - col_off[i]
            home = (spot // cells + MAXOFF - row_off[i]) * rows + col * own + i
            pick = one_hot(jnp.where((col >= 0) & (col < cells), home, GONE), source.shape[0])
            df_ref[i] = dot(pick, source, 1, 0).astype(BF16)

    restore(range(own // 2))
    for copy in line_copies:
        copy.wait()
    total = second[chip].astype(F32)
    for k in range(1, chips):
        total = total + line_in[k].astype(F32)
    final[...] = total.astype(BF16)
    every[me] = total.astype(BF16)
    every_copies = [sender(final, every.at[me], every_sem, k, (peers[k], tile)) for k in range(1, parts)]
    for copy in every_copies:
        copy.start()
    restore(range(own // 2, own - 1))
    for copy in every_copies:
        copy.wait()
    whole = every[...].astype(F32)
    summed = jnp.sum(whole * whole, axis=0)
    summed = jnp.sum(jnp.sum(summed, axis=0, keepdims=True), axis=1, keepdims=True)
    level = jnp.broadcast_to(summed, (8, 128))
    square[...] = level
    squares[tile] = level
    square_copies = [
        sender(square, squares.at[tile], square_sem, k, (me, lax.rem(tile + k, tiles))) for k in range(1, tiles)
    ]
    for copy in square_copies:
        copy.start()
    restore(range(own - 1, own))
    for copy in square_copies:
        copy.wait()
    norm = jnp.sqrt(jnp.sum(squares[...], axis=0)[:1, :1])
    limit = math.sqrt(8.0 * channels * channels)
    factor = limit / jnp.maximum(norm, limit)
    for t in range(2):
        for j in range(4):
            piece = every[j].astype(F32)[t * share:(t + 1) * share] * factor
            if j < 3:
                gq_ref[t, :, j * channels:(j + 1) * channels] = piece
            else:
                go_ref[t] = piece


def body(feats, types, valid, offsets, w_qkv, w_out, d_out):
    own, row_count, cells, channels = feats.shape
    parts = lax.axis_size("agent")
    tiles = lax.axis_size("tile")
    assert row_count == parts == 4
    agents = own * parts
    local = row_count * cells
    inner = local + 2 * MAXOFF * cells
    rows = cells * own
    n = cells * agents
    chips = tiles // 2
    share = channels // tiles
    block = pltpu.VMEM((parts, rows, channels), BF16)
    pieces = pltpu.VMEM((4, chips, 2 * share, channels), BF16)
    line = pltpu.VMEM((chips, 2 * share, channels), BF16)

    def dma(count):
        return pltpu.SemaphoreType.DMA((2, count))

    d_feats, g_qkv, g_out = pl.pallas_call(
        functools.partial(kernel, parts, tiles, agents),
        out_shape=(
            jax.ShapeDtypeStruct((own, local, channels), BF16),
            jax.ShapeDtypeStruct((2, share, 3 * channels), F32),
            jax.ShapeDtypeStruct((2, share, channels), F32),
        ),
        in_specs=[HBM, SMEM, SMEM, SMEM, HBM, HBM, HBM],
        out_specs=(VMEM,) * 3,
        scratch_shapes=[
            pltpu.VMEM((own, inner, channels), BF16),
            pltpu.VMEM((own, local, channels), BF16),
            pltpu.VMEM(w_qkv.shape, BF16),
            pltpu.VMEM(w_out.shape, BF16),
            block, block, block, block,
            pltpu.VMEM((n, channels), BF16),
            pltpu.VMEM((n, channels), BF16),
            pltpu.VMEM((n, 3 * channels), BF16),
            pltpu.VMEM((n, channels), BF16),
            pltpu.VMEM((n, channels), BF16),
            pltpu.VMEM((n, 3 * channels), BF16),
            pltpu.VMEM((HEADS * agents, channels), BF16),
            block,
            pltpu.VMEM((2, 4, chips, 2 * share, channels), BF16),
            pltpu.VMEM((parts + 2 * MAXOFF, rows, channels), BF16),
            pieces, pieces,
            pltpu.VMEM((parts, chips, 2 * share, channels), BF16),
            line, line,
            pltpu.VMEM((2 * share, channels), BF16),
            pltpu.VMEM((parts, 2 * share, channels), BF16),
            pltpu.VMEM((8, 128), F32),
            pltpu.VMEM((tiles, 8, 128), F32),
            pltpu.SemaphoreType.DMA((4,)),
            dma(2), dma(parts), dma(parts), dma(parts), dma(2), dma(1), dma(parts), dma(chips), dma(parts), dma(tiles),
        ],
        compiler_params=pltpu.CompilerParams(
            collective_id=0, has_side_effects=True, vmem_limit_bytes=48 * 2**20
        ),
    )(feats.reshape(own, local, channels), types, valid, offsets, w_qkv, w_out, d_out.reshape(own, local, channels))
    return (d_feats.reshape(feats.shape), g_qkv, g_out)


def solution(mesh):
    placed = (
        P("agent", "tile", None, None),
        P(),
        P(),
        P(),
        P(),
        P(),
        P("agent", "tile", None, None),
    )
    return jax.shard_map(
        body,
        mesh=mesh,
        in_specs=placed,
        out_specs=(P("agent", "tile", None, None), P(None, "tile", None), P(None, "tile", None)),
        check_vma=False,
    )
```

```python
import functools
import math

import jax
import jax.numpy as jnp
from jax import lax
from jax.experimental import pallas as pl
from jax.experimental.pallas import tpu as pltpu
from jax.sharding import PartitionSpec as P

HEADS = 8
MAXOFF = 2
F32 = jnp.float32
BF16 = jnp.bfloat16


def dot(a, b, ca, cb):
    return lax.dot_general(a, b, (((ca,), (cb,)), ((), ())), preferred_element_type=F32)


VMEM = pl.BlockSpec(memory_space=pltpu.VMEM)
HBM = pl.BlockSpec(memory_space=pltpu.HBM)
SMEM = pl.BlockSpec(memory_space=pltpu.SMEM)
MESH = pl.DeviceIdType.MESH
GONE = -(1 << 20)


def one_hot(target, width):
    lanes = lax.broadcasted_iota(jnp.int32, (target.shape[0], width), 1)
    return jnp.where(lanes == target, 1.0, 0.0).astype(BF16)


def greet(others):
    barrier = pltpu.get_barrier_semaphore()
    for there, device in others:
        @pl.when(there)
        def _(device=device):
            pl.semaphore_signal(barrier, inc=1, device_id=device, device_id_type=MESH)
    count = sum(jnp.where(there, 1, 0) for there, _ in others)
    pl.semaphore_wait(barrier, count)


def sender(src, dst, sems, k, device):
    return pltpu.make_async_remote_copy(
        src_ref=src, dst_ref=dst, send_sem=sems.at[0, k], recv_sem=sems.at[1, k], device_id=device, device_id_type=MESH
    )


def spelled(index, values):
    out = jnp.zeros_like(index)
    for j, value in enumerate(values):
        out = jnp.where(index == j, value, out)
    return out


def kernel(parts, tiles, agents, feats_ref, types_ref, valid_ref, offs_ref, wqkv_hbm, wout_hbm, grads_hbm,
           df_ref, gq_ref, go_ref,
           rim, grads, warped, wqkv_ref, wout_ref, x_send, g_send, x_recv, g_recv, x_ref, g_ref,
           qkv_s, da_s, att_s, dqkv_s, head_s, dx, dx_send, raw, back_rim, pair, first, agent_in, second, line_in,
           final, every, square, squares,
           load_sem, halo_sem, x_sem, g_sem, dx_sem, side_sem, pair_sem, agent_sem, line_sem, every_sem, square_sem):
    me, tile = lax.axis_index("agent"), lax.axis_index("tile")
    core, chip = lax.rem(tile, 2), tile // 2
    chips = tiles // 2
    own, local, channels = feats_ref.shape
    cells = local // parts
    edge = MAXOFF * cells
    inner = rim.shape[1]
    left, right = tile > 0, tile < tiles - 1
    always = parts > 0
    peers = [lax.rem(me + k, parts) for k in range(parts)]

    loads = [
        pltpu.make_async_copy(grads_hbm, grads, load_sem.at[0]),
        pltpu.make_async_copy(feats_ref, rim.at[:, edge:inner - edge, :], load_sem.at[1]),
        pltpu.make_async_copy(wout_hbm, wout_ref, load_sem.at[2]),
        pltpu.make_async_copy(wqkv_hbm, wqkv_ref, load_sem.at[3]),
    ]
    for copy in loads:
        copy.start()
    greet(
        [(always, (peers[k], tile)) for k in range(1, parts)]
        + [(always, (me, lax.rem(tile + k, tiles))) for k in range(1, tiles)]
    )
    to_right = sender(feats_ref.at[:, local - edge:, :], rim.at[:, :edge, :], halo_sem, 0, (me, tile + 1))
    to_left = sender(feats_ref.at[:, :edge, :], rim.at[:, inner - edge:, :], halo_sem, 1, (me, tile - 1))

    @pl.when(right)
    def _():
        to_right.start()

    @pl.when(left)
    def _():
        to_left.start()

    rows = cells * own

    @pl.when(tile == 0)
    def _():
        rim[:, :edge, :] = jnp.zeros((own, edge, channels), BF16)
        back_rim[:MAXOFF] = jnp.zeros((MAXOFF, own, cells, channels), BF16)

    @pl.when(tile == tiles - 1)
    def _():
        rim[:, inner - edge:, :] = jnp.zeros((own, edge, channels), BF16)
        back_rim[parts + MAXOFF:] = jnp.zeros((MAXOFF, own, cells, channels), BF16)

    place = lax.broadcasted_iota(jnp.int32, (rows, 1), 0)
    to_cells = one_hot((place % own) * cells + place // own, rows)
    to_agents = one_hot((place % cells) * own + place // cells, rows)
    spot = lax.broadcasted_iota(jnp.int32, (local, 1), 0)
    row_off = [offs_ref[me * own + j, 0] for j in range(own)]
    col_off = [offs_ref[me * own + j, 1] for j in range(own)]

    def shift(i, direction):
        col = spot % cells + direction * col_off[i]
        target = (spot // cells + MAXOFF + direction * row_off[i]) * cells + col
        return one_hot(jnp.where((col >= 0) & (col < cells), target, GONE), inner)

    def spread(source, send, recv, sems):
        copies = []
        for k in (*range(1, parts), 0):
            part = source[:, peers[k]].astype(F32).reshape(rows, channels).astype(BF16)
            value = dot(to_cells, part, 1, 0).astype(BF16)
            if k == 0:
                recv[me] = value
            else:
                send[k] = value
                copies.append(sender(send.at[k], recv.at[me], sems, k, (peers[k], tile)))
                copies[-1].start()
        return copies

    def gather(copies, recv, out):
        for copy in copies:
            copy.wait()
        pieces = [recv[n].astype(F32).reshape(cells, own, channels) for n in range(parts)]
        out[...] = jnp.concatenate(pieces, axis=1).reshape(rows * parts, channels).astype(BF16)

    loads[0].wait()
    g_copies = spread(grads, g_send, g_recv, g_sem)
    loads[1].wait()

    @pl.when(left)
    def _():
        to_right.wait_recv()
        to_left.wait_send()

    @pl.when(right)
    def _():
        to_left.wait_recv()
        to_right.wait_send()

    for i in range(own):
        warped[i] = dot(shift(i, 1), rim[i], 1, 0).reshape(parts, cells, channels)
    x_copies = spread(warped, x_send, x_recv, x_sem)

    size = channels // HEADS
    scale = size ** (-0.5)
    wide = HEADS * agents
    group = 8
    span = group * agents
    agent_col = lax.broadcasted_iota(jnp.int32, (agents, 1), 0)
    kind = spelled(agent_col, [types_ref[j] for j in range(agents)])
    valid = spelled(agent_col, [valid_ref[j] for j in range(agents)])
    type_wide = jnp.broadcast_to(kind, (agents, channels)).astype(F32)
    type_rows = jnp.concatenate([type_wide] * group, axis=0)
    owner = lax.broadcasted_iota(jnp.int32, (wide, channels), 0) // agents
    lane = lax.broadcasted_iota(jnp.int32, (wide, channels), 1) // size
    head_s[...] = jnp.where(owner == lane, 1.0, 0.0).astype(BF16)

    loads[2].wait()
    loads[3].wait()
    gather(g_copies, g_recv, g_ref)

    def project_g(i, _):
        at = pl.ds(pl.multiple_of(i * span, span), span)
        g = g_ref[at, :]
        a = dot(g, wout_ref[0], 1, 1)
        b = dot(g, wout_ref[1], 1, 1)
        da_s[at, :] = jnp.where(type_rows > 0.5, b, a).astype(BF16)
        return 0

    lax.fori_loop(0, cells // group, project_g, 0)
    gather(x_copies, x_recv, x_ref)

    def project(i, _):
        at = pl.ds(pl.multiple_of(i * span, span), span)
        x = x_ref[at, :]
        for j in range(3):
            cols = slice(j * channels, (j + 1) * channels)
            a = dot(x, wqkv_ref[0, :, cols], 1, 0)
            b = dot(x, wqkv_ref[1, :, cols], 1, 0)
            qkv_s[at, cols] = jnp.where(type_rows > 0.5, b, a).astype(BF16)
        return 0

    lax.fori_loop(0, cells // group, project, 0)

    key_id = lax.broadcasted_iota(jnp.int32, (agents, wide), 0)
    query_id = lax.broadcasted_iota(jnp.int32, (agents, wide), 1) % agents
    allowed = (jnp.broadcast_to(valid, (agents, wide)) == 1) | (key_id == query_id)
    lane_head = lax.broadcasted_iota(jnp.int32, (agents, channels), 1) // size

    def own_heads(full):
        out = full[:agents]
        for h in range(1, HEADS):
            out = jnp.where(lane_head == h, full[h * agents:(h + 1) * agents], out)
        return out

    def attend(i, _):
        at = pl.ds(pl.multiple_of(i * agents, agents), agents)
        q = qkv_s[at, :channels]
        k = qkv_s[at, channels:2 * channels]
        v = qkv_s[at, 2 * channels:]
        da = da_s[at, :]
        mask = head_s[...]
        qx = jnp.concatenate([q] * HEADS, axis=0) * mask
        dax = jnp.concatenate([da] * HEADS, axis=0) * mask
        scores = dot(k, qx, 1, 1) * scale
        raised = jnp.where(allowed, jnp.exp(scores), 0.0)
        prob = raised / jnp.sum(raised, axis=0, keepdims=True)
        low = prob.astype(BF16)
        pg = dot(v, dax, 1, 1)
        sg = (prob * (pg - jnp.sum(prob * pg, axis=0, keepdims=True)) * scale).astype(BF16)
        dqkv_s[at, channels:2 * channels] = dot(sg, qx, 1, 0).astype(BF16)
        dqkv_s[at, 2 * channels:] = dot(low, dax, 1, 0).astype(BF16)
        att_s[at, :] = own_heads(dot(low, v, 0, 0)).astype(BF16)
        dqkv_s[at, :channels] = own_heads(dot(sg, k, 0, 0)).astype(BF16)
        return 0

    lax.fori_loop(0, cells, attend, 0, unroll=4)

    share = channels // tiles
    ones = jnp.concatenate([type_wide.astype(BF16)] * cells, axis=0)
    for t in range(2):
        pick = ones if t else (1 - ones).astype(BF16)
        xt = x_ref[...] * pick
        for j in range(4):
            if j < 3:
                full = dot(xt, dqkv_s[:, j * channels:(j + 1) * channels], 0, 0)
            else:
                full = dot(att_s[...] * pick, g_ref[...], 0, 0)
            for i in range(tiles):
                raw[i % 2, j, i // 2, t * share:(t + 1) * share, :] = full[i * share:(i + 1) * share].astype(BF16)
    swap = sender(raw.at[1 - core], pair, pair_sem, 0, (me, tile + 1 - 2 * core))
    swap.start()

    def back(i, _):
        at = pl.ds(pl.multiple_of(i * span, span), span)
        d = dqkv_s[at, :]
        a = dot(d, wqkv_ref[0], 1, 1)
        b = dot(d, wqkv_ref[1], 1, 1)
        full = jnp.where(type_rows > 0.5, b, a).reshape(group, agents, channels)
        for n in range(parts):
            part = full[:, n * own:(n + 1) * own].reshape(group * own, channels)
            dx[n, pl.ds(pl.multiple_of(i * group * own, group * own), group * own), :] = part.astype(BF16)
        return 0

    lax.fori_loop(0, cells // group, back, 0)
    homes = []
    for k in (*range(1, parts), 0):
        value = dot(to_agents, dx[peers[k]], 1, 0).reshape(own, cells, channels).astype(BF16)
        if k == 0:
            back_rim[me + MAXOFF] = value
        else:
            dx_send[k] = value
            homes.append(sender(dx_send.at[k], back_rim.at[me + MAXOFF], dx_sem, k, (peers[k], tile)))
            homes[-1].start()

    swap.wait()
    first[...] = (raw[core].astype(F32) + pair[...].astype(F32)).astype(BF16)
    agent_copies = [sender(first.at[peers[k]], agent_in.at[k], agent_sem, k, (peers[k], tile)) for k in range(1, parts)]
    for copy in agent_copies:
        copy.start()

    for copy in homes:
        copy.wait()
    side_left = sender(
        back_rim.at[MAXOFF:2 * MAXOFF], back_rim.at[parts + MAXOFF:], side_sem, 0, (me, tile - 1)
    )
    side_right = sender(back_rim.at[parts:parts + MAXOFF], back_rim.at[:MAXOFF], side_sem, 1, (me, tile + 1))

    @pl.when(left)
    def _():
        side_left.start()

    @pl.when(right)
    def _():
        side_right.start()

    for copy in agent_copies:
        copy.wait()
    total = first[me].astype(F32)
    for k in range(1, parts):
        total = total + agent_in[k].astype(F32)
    second[...] = total.astype(BF16)
    line_copies = []
    for k in range(1, chips):
        other = lax.rem(chip + k, chips)
        line_copies.append(sender(second.at[other], line_in.at[k], line_sem, k, (me, 2 * other + core)))
        line_copies[-1].start()

    @pl.when(left)
    def _():
        side_right.wait_recv()
        side_left.wait_send()

    @pl.when(right)
    def _():
        side_left.wait_recv()
        side_right.wait_send()

    def restore(agent_ids):
        for i in agent_ids:
            source = back_rim[:, i].astype(F32).reshape(inner, channels).astype(BF16)
            df_ref[i] = dot(shift(i, -1), source, 1, 0).astype(BF16)

    restore(range(own // 2))
    for copy in line_copies:
        copy.wait()
    total = second[chip].astype(F32)
    for k in range(1, chips):
        total = total + line_in[k].astype(F32)
    final[...] = total.astype(BF16)
    every[me] = total.astype(BF16)
    every_copies = [sender(final, every.at[me], every_sem, k, (peers[k], tile)) for k in range(1, parts)]
    for copy in every_copies:
        copy.start()
    restore(range(own // 2, own - 1))
    for copy in every_copies:
        copy.wait()
    whole = every[...].astype(F32)
    summed = jnp.sum(whole * whole, axis=0)
    summed = jnp.sum(jnp.sum(summed, axis=0, keepdims=True), axis=1, keepdims=True)
    level = jnp.broadcast_to(summed, (8, 128))
    square[...] = level
    squares[tile] = level
    square_copies = [
        sender(square, squares.at[tile], square_sem, k, (me, lax.rem(tile + k, tiles))) for k in range(1, tiles)
    ]
    for copy in square_copies:
        copy.start()
    restore(range(own - 1, own))
    for copy in square_copies:
        copy.wait()
    norm = jnp.sqrt(jnp.sum(squares[...], axis=0)[:1, :1])
    limit = math.sqrt(8.0 * channels * channels)
    factor = limit / jnp.maximum(norm, limit)
    for t in range(2):
        for j in range(4):
            piece = every[j].astype(F32)[t * share:(t + 1) * share] * factor
            if j < 3:
                gq_ref[t, :, j * channels:(j + 1) * channels] = piece
            else:
                go_ref[t] = piece


def body(feats, types, valid, offsets, w_qkv, w_out, d_out):
    own, row_count, cells, channels = feats.shape
    parts = lax.axis_size("agent")
    tiles = lax.axis_size("tile")
    assert row_count == parts == 4
    agents = own * parts
    local = row_count * cells
    inner = local + 2 * MAXOFF * cells
    rows = cells * own
    n = cells * agents
    chips = tiles // 2
    share = channels // tiles
    block = pltpu.VMEM((parts, rows, channels), BF16)
    pieces = pltpu.VMEM((4, chips, 2 * share, channels), BF16)
    line = pltpu.VMEM((chips, 2 * share, channels), BF16)

    def dma(count):
        return pltpu.SemaphoreType.DMA((2, count))

    d_feats, g_qkv, g_out = pl.pallas_call(
        functools.partial(kernel, parts, tiles, agents),
        out_shape=(
            jax.ShapeDtypeStruct((own, local, channels), BF16),
            jax.ShapeDtypeStruct((2, share, 3 * channels), F32),
            jax.ShapeDtypeStruct((2, share, channels), F32),
        ),
        in_specs=[HBM, SMEM, SMEM, SMEM, HBM, HBM, HBM],
        out_specs=(VMEM,) * 3,
        scratch_shapes=[
            pltpu.VMEM((own, inner, channels), BF16),
            pltpu.VMEM((own, parts, cells, channels), BF16),
            pltpu.VMEM((own, parts, cells, channels), F32),
            pltpu.VMEM(w_qkv.shape, BF16),
            pltpu.VMEM(w_out.shape, BF16),
            block, block, block, block,
            pltpu.VMEM((n, channels), BF16),
            pltpu.VMEM((n, channels), BF16),
            pltpu.VMEM((n, 3 * channels), BF16),
            pltpu.VMEM((n, channels), BF16),
            pltpu.VMEM((n, channels), BF16),
            pltpu.VMEM((n, 3 * channels), BF16),
            pltpu.VMEM((HEADS * agents, channels), BF16),
            block,
            pltpu.VMEM((parts, own, cells, channels), BF16),
            pltpu.VMEM((2, 4, chips, 2 * share, channels), BF16),
            pltpu.VMEM((parts + 2 * MAXOFF, own, cells, channels), BF16),
            pieces, pieces,
            pltpu.VMEM((parts, chips, 2 * share, channels), BF16),
            line, line,
            pltpu.VMEM((2 * share, channels), BF16),
            pltpu.VMEM((parts, 2 * share, channels), BF16),
            pltpu.VMEM((8, 128), F32),
            pltpu.VMEM((tiles, 8, 128), F32),
            pltpu.SemaphoreType.DMA((4,)),
            dma(2), dma(parts), dma(parts), dma(parts), dma(2), dma(1), dma(parts), dma(chips), dma(parts), dma(tiles),
        ],
        compiler_params=pltpu.CompilerParams(
            collective_id=0, has_side_effects=True, vmem_limit_bytes=48 * 2**20
        ),
    )(feats.reshape(own, local, channels), types, valid, offsets, w_qkv, w_out, d_out)
    return (d_feats.reshape(feats.shape), g_qkv, g_out)


def solution(mesh):
    placed = (
        P("agent", "tile", None, None),
        P(),
        P(),
        P(),
        P(),
        P(),
        P("agent", "tile", None, None),
    )
    return jax.shard_map(
        body,
        mesh=mesh,
        in_specs=placed,
        out_specs=(P("agent", "tile", None, None), P(None, "tile", None), P(None, "tile", None)),
        check_vma=False,
    )
```

```python
import functools
import math

import jax
import jax.numpy as jnp
from jax import lax
from jax.experimental import pallas as pl
from jax.experimental.pallas import tpu as pltpu
from jax.sharding import PartitionSpec as P

HEADS = 8
MAXOFF = 2
F32 = jnp.float32
BF16 = jnp.bfloat16


def dot(a, b, ca, cb):
    return lax.dot_general(a, b, (((ca,), (cb,)), ((), ())), preferred_element_type=F32)


VMEM = pl.BlockSpec(memory_space=pltpu.VMEM)
HBM = pl.BlockSpec(memory_space=pltpu.HBM)
SMEM = pl.BlockSpec(memory_space=pltpu.SMEM)
MESH = pl.DeviceIdType.MESH
GONE = -(1 << 20)


def one_hot(target, width):
    lanes = lax.broadcasted_iota(jnp.int32, (target.shape[0], width), 1)
    return jnp.where(lanes == target, 1.0, 0.0).astype(BF16)


def greet(others):
    barrier = pltpu.get_barrier_semaphore()
    for there, device in others:
        @pl.when(there)
        def _(device=device):
            pl.semaphore_signal(barrier, inc=1, device_id=device, device_id_type=MESH)
    count = sum(jnp.where(there, 1, 0) for there, _ in others)
    pl.semaphore_wait(barrier, count)


def sender(src, dst, sems, k, device):
    return pltpu.make_async_remote_copy(
        src_ref=src, dst_ref=dst, send_sem=sems.at[0, k], recv_sem=sems.at[1, k], device_id=device, device_id_type=MESH
    )


def spelled(index, values):
    out = jnp.zeros_like(index)
    for j, value in enumerate(values):
        out = jnp.where(index == j, value, out)
    return out


def kernel(parts, tiles, agents, feats_ref, types_ref, valid_ref, offs_ref, wqkv_hbm, wout_hbm, grads_hbm,
           df_ref, gq_ref, go_ref,
           rim, grads, warped, wqkv_ref, wout_ref, x_send, g_send, x_recv, g_recv, x_ref, g_ref,
           qkv_s, da_s, att_s, dqkv_s, head_s, dx, dx_send, raw, back_rim, pair, first, agent_in, second, line_in,
           final, every, square, squares,
           load_sem, halo_sem, x_sem, g_sem, dx_sem, side_sem, pair_sem, agent_sem, line_sem, every_sem, square_sem):
    me, tile = lax.axis_index("agent"), lax.axis_index("tile")
    core, chip = lax.rem(tile, 2), tile // 2
    chips = tiles // 2
    own, local, channels = feats_ref.shape
    cells = local // parts
    edge = MAXOFF * cells
    inner = rim.shape[1]
    left, right = tile > 0, tile < tiles - 1
    always = parts > 0
    peers = [lax.rem(me + k, parts) for k in range(parts)]

    loads = [
        pltpu.make_async_copy(grads_hbm, grads, load_sem.at[0]),
        pltpu.make_async_copy(feats_ref, rim.at[:, edge:inner - edge, :], load_sem.at[1]),
        pltpu.make_async_copy(wout_hbm, wout_ref, load_sem.at[2]),
        pltpu.make_async_copy(wqkv_hbm, wqkv_ref, load_sem.at[3]),
    ]
    for copy in loads:
        copy.start()
    greet(
        [(always, (peers[k], tile)) for k in range(1, parts)]
        + [(always, (me, lax.rem(tile + k, tiles))) for k in range(1, tiles)]
    )
    to_right = sender(feats_ref.at[:, local - edge:, :], rim.at[:, :edge, :], halo_sem, 0, (me, tile + 1))
    to_left = sender(feats_ref.at[:, :edge, :], rim.at[:, inner - edge:, :], halo_sem, 1, (me, tile - 1))

    @pl.when(right)
    def _():
        to_right.start()

    @pl.when(left)
    def _():
        to_left.start()

    rows = cells * own

    @pl.when(tile == 0)
    def _():
        rim[:, :edge, :] = jnp.zeros((own, edge, channels), BF16)
        back_rim[:MAXOFF] = jnp.zeros((MAXOFF, own, cells, channels), BF16)

    @pl.when(tile == tiles - 1)
    def _():
        rim[:, inner - edge:, :] = jnp.zeros((own, edge, channels), BF16)
        back_rim[parts + MAXOFF:] = jnp.zeros((MAXOFF, own, cells, channels), BF16)

    place = lax.broadcasted_iota(jnp.int32, (rows, 1), 0)
    to_cells = one_hot((place % own) * cells + place // own, rows)
    to_agents = one_hot((place % cells) * own + place // cells, rows)
    spot = lax.broadcasted_iota(jnp.int32, (local, 1), 0)
    row_off = [offs_ref[me * own + j, 0] for j in range(own)]
    col_off = [offs_ref[me * own + j, 1] for j in range(own)]

    def shift(i, direction):
        col = spot % cells + direction * col_off[i]
        target = (spot // cells + MAXOFF + direction * row_off[i]) * cells + col
        return one_hot(jnp.where((col >= 0) & (col < cells), target, GONE), inner)

    def spread(source, send, recv, sems):
        copies = []
        for k in (*range(1, parts), 0):
            part = source[:, peers[k]].astype(F32).reshape(rows, channels).astype(BF16)
            value = dot(to_cells, part, 1, 0).astype(BF16)
            if k == 0:
                recv[me] = value
            else:
                send[k] = value
                copies.append(sender(send.at[k], recv.at[me], sems, k, (peers[k], tile)))
                copies[-1].start()
        return copies

    def gather(copies, recv, out):
        for copy in copies:
            copy.wait()
        pieces = [recv[n].astype(F32).reshape(cells, own, channels) for n in range(parts)]
        out[...] = jnp.concatenate(pieces, axis=1).reshape(rows * parts, channels).astype(BF16)

    loads[0].wait()
    g_copies = spread(grads, g_send, g_recv, g_sem)
    loads[1].wait()

    @pl.when(left)
    def _():
        to_right.wait_recv()
        to_left.wait_send()

    @pl.when(right)
    def _():
        to_left.wait_recv()
        to_right.wait_send()

    for i in range(own):
        warped[i] = dot(shift(i, 1), rim[i], 1, 0).reshape(parts, cells, channels)
    x_copies = spread(warped, x_send, x_recv, x_sem)

    size = channels // HEADS
    scale = size ** (-0.5)
    wide = HEADS * agents
    group = 8
    span = group * agents
    agent_col = lax.broadcasted_iota(jnp.int32, (agents, 1), 0)
    kind = spelled(agent_col, [types_ref[j] for j in range(agents)])
    valid = spelled(agent_col, [valid_ref[j] for j in range(agents)])
    type_wide = jnp.broadcast_to(kind, (agents, channels)).astype(F32)
    type_rows = jnp.concatenate([type_wide] * group, axis=0)
    owner = lax.broadcasted_iota(jnp.int32, (wide, channels), 0) // agents
    lane = lax.broadcasted_iota(jnp.int32, (wide, channels), 1) // size
    head_s[...] = jnp.where(owner == lane, 1.0, 0.0).astype(BF16)

    loads[2].wait()
    loads[3].wait()
    gather(g_copies, g_recv, g_ref)

    def project_g(i, _):
        at = pl.ds(pl.multiple_of(i * span, span), span)
        g = g_ref[at, :]
        a = dot(g, wout_ref[0], 1, 1)
        b = dot(g, wout_ref[1], 1, 1)
        da_s[at, :] = jnp.where(type_rows > 0.5, b, a).astype(BF16)
        return 0

    lax.fori_loop(0, cells // group, project_g, 0)
    gather(x_copies, x_recv, x_ref)

    def project(i, _):
        at = pl.ds(pl.multiple_of(i * span, span), span)
        x = x_ref[at, :]
        for j in range(3):
            cols = slice(j * channels, (j + 1) * channels)
            a = dot(x, wqkv_ref[0, :, cols], 1, 0)
            b = dot(x, wqkv_ref[1, :, cols], 1, 0)
            qkv_s[at, cols] = jnp.where(type_rows > 0.5, b, a).astype(BF16)
        return 0

    lax.fori_loop(0, cells // group, project, 0)

    key_id = lax.broadcasted_iota(jnp.int32, (agents, wide), 0)
    query_id = lax.broadcasted_iota(jnp.int32, (agents, wide), 1) % agents
    allowed = (jnp.broadcast_to(valid, (agents, wide)) == 1) | (key_id == query_id)
    lane_head = lax.broadcasted_iota(jnp.int32, (agents, channels), 1) // size

    def own_heads(full):
        out = full[:agents]
        for h in range(1, HEADS):
            out = jnp.where(lane_head == h, full[h * agents:(h + 1) * agents], out)
        return out

    def attend(i, _):
        at = pl.ds(pl.multiple_of(i * agents, agents), agents)
        q = qkv_s[at, :channels]
        k = qkv_s[at, channels:2 * channels]
        v = qkv_s[at, 2 * channels:]
        da = da_s[at, :]
        mask = head_s[...]
        qx = jnp.concatenate([q] * HEADS, axis=0) * mask
        dax = jnp.concatenate([da] * HEADS, axis=0) * mask
        scores = dot(k, qx, 1, 1) * scale
        raised = jnp.where(allowed, jnp.exp(scores), 0.0)
        prob = raised / jnp.sum(raised, axis=0, keepdims=True)
        low = prob.astype(BF16)
        pg = dot(v, dax, 1, 1)
        sg = (prob * (pg - jnp.sum(prob * pg, axis=0, keepdims=True)) * scale).astype(BF16)
        dqkv_s[at, channels:2 * channels] = dot(sg, qx, 1, 0).astype(BF16)
        dqkv_s[at, 2 * channels:] = dot(low, dax, 1, 0).astype(BF16)
        att_s[at, :] = own_heads(dot(low, v, 0, 0)).astype(BF16)
        dqkv_s[at, :channels] = own_heads(dot(sg, k, 0, 0)).astype(BF16)
        return 0

    lax.fori_loop(0, cells, attend, 0, unroll=4)

    share = channels // tiles
    ones = jnp.concatenate([type_wide.astype(BF16)] * cells, axis=0)
    for t in range(2):
        pick = ones if t else (1 - ones).astype(BF16)
        xt = x_ref[...] * pick
        for j in range(4):
            if j < 3:
                full = dot(xt, dqkv_s[:, j * channels:(j + 1) * channels], 0, 0)
            else:
                full = dot(att_s[...] * pick, g_ref[...], 0, 0)
            for i in range(tiles):
                raw[i % 2, j, i // 2, t * share:(t + 1) * share, :] = full[i * share:(i + 1) * share].astype(BF16)
    swap = sender(raw.at[1 - core], pair, pair_sem, 0, (me, tile + 1 - 2 * core))
    swap.start()

    def back(i, _):
        at = pl.ds(pl.multiple_of(i * span, span), span)
        d = dqkv_s[at, :]
        a = dot(d, wqkv_ref[0], 1, 1)
        b = dot(d, wqkv_ref[1], 1, 1)
        full = jnp.where(type_rows > 0.5, b, a).reshape(group, agents, channels)
        for n in range(parts):
            part = full[:, n * own:(n + 1) * own].reshape(group * own, channels)
            dx[n, pl.ds(pl.multiple_of(i * group * own, group * own), group * own), :] = part.astype(BF16)
        return 0

    lax.fori_loop(0, cells // group, back, 0)
    homes = []
    for k in (*range(1, parts), 0):
        value = dot(to_agents, dx[peers[k]], 1, 0).reshape(own, cells, channels).astype(BF16)
        if k == 0:
            back_rim[me + MAXOFF] = value
        else:
            dx_send[k] = value
            homes.append(sender(dx_send.at[k], back_rim.at[me + MAXOFF], dx_sem, k, (peers[k], tile)))
            homes[-1].start()

    swap.wait()
    first[...] = (raw[core].astype(F32) + pair[...].astype(F32)).astype(BF16)
    agent_copies = [sender(first.at[peers[k]], agent_in.at[k], agent_sem, k, (peers[k], tile)) for k in range(1, parts)]
    for copy in agent_copies:
        copy.start()

    for copy in homes:
        copy.wait()
    side_left = sender(
        back_rim.at[MAXOFF:2 * MAXOFF], back_rim.at[parts + MAXOFF:], side_sem, 0, (me, tile - 1)
    )
    side_right = sender(back_rim.at[parts:parts + MAXOFF], back_rim.at[:MAXOFF], side_sem, 1, (me, tile + 1))

    @pl.when(left)
    def _():
        side_left.start()

    @pl.when(right)
    def _():
        side_right.start()

    for copy in agent_copies:
        copy.wait()
    total = first[me].astype(F32)
    for k in range(1, parts):
        total = total + agent_in[k].astype(F32)
    second[...] = total.astype(BF16)
    line_copies = []
    for k in range(1, chips):
        other = lax.rem(chip + k, chips)
        line_copies.append(sender(second.at[other], line_in.at[k], line_sem, k, (me, 2 * other + core)))
        line_copies[-1].start()

    @pl.when(left)
    def _():
        side_right.wait_recv()
        side_left.wait_send()

    @pl.when(right)
    def _():
        side_left.wait_recv()
        side_right.wait_send()

    def restore(agent_ids):
        for i in agent_ids:
            source = back_rim[:, i].astype(F32).reshape(inner, channels).astype(BF16)
            df_ref[i] = dot(shift(i, -1), source, 1, 0).astype(BF16)

    restore(range(own // 2))
    for copy in line_copies:
        copy.wait()
    total = second[chip].astype(F32)
    for k in range(1, chips):
        total = total + line_in[k].astype(F32)
    final[...] = total.astype(BF16)
    every[me] = total.astype(BF16)
    every_copies = [sender(final, every.at[me], every_sem, k, (peers[k], tile)) for k in range(1, parts)]
    for copy in every_copies:
        copy.start()
    restore(range(own // 2, own - 1))
    for copy in every_copies:
        copy.wait()
    whole = every[...].astype(F32)
    summed = jnp.sum(whole * whole, axis=0)
    summed = jnp.sum(jnp.sum(summed, axis=0, keepdims=True), axis=1, keepdims=True)
    level = jnp.broadcast_to(summed, (8, 128))
    square[...] = level
    squares[tile] = level
    square_copies = [
        sender(square, squares.at[tile], square_sem, k, (me, lax.rem(tile + k, tiles))) for k in range(1, tiles)
    ]
    for copy in square_copies:
        copy.start()
    restore(range(own - 1, own))
    for copy in square_copies:
        copy.wait()
    norm = jnp.sqrt(jnp.sum(squares[...], axis=0)[:1, :1])
    limit = math.sqrt(8.0 * channels * channels)
    factor = limit / jnp.maximum(norm, limit)
    for t in range(2):
        for j in range(4):
            piece = every[j].astype(F32)[t * share:(t + 1) * share] * factor
            if j < 3:
                gq_ref[t, :, j * channels:(j + 1) * channels] = piece
            else:
                go_ref[t] = piece


def body(feats, types, valid, offsets, w_qkv, w_out, d_out):
    own, row_count, cells, channels = feats.shape
    parts = lax.axis_size("agent")
    tiles = lax.axis_size("tile")
    assert row_count == parts == 4
    agents = own * parts
    local = row_count * cells
    inner = local + 2 * MAXOFF * cells
    rows = cells * own
    n = cells * agents
    chips = tiles // 2
    share = channels // tiles
    block = pltpu.VMEM((parts, rows, channels), BF16)
    pieces = pltpu.VMEM((4, chips, 2 * share, channels), BF16)
    line = pltpu.VMEM((chips, 2 * share, channels), BF16)

    def dma(count):
        return pltpu.SemaphoreType.DMA((2, count))

    d_feats, g_qkv, g_out = pl.pallas_call(
        functools.partial(kernel, parts, tiles, agents),
        out_shape=(
            jax.ShapeDtypeStruct((own, local, channels), BF16),
            jax.ShapeDtypeStruct((2, share, 3 * channels), F32),
            jax.ShapeDtypeStruct((2, share, channels), F32),
        ),
        in_specs=[HBM, SMEM, SMEM, SMEM, HBM, HBM, HBM],
        out_specs=(VMEM,) * 3,
        scratch_shapes=[
            pltpu.VMEM((own, inner, channels), BF16),
            pltpu.VMEM((own, parts, cells, channels), BF16),
            pltpu.VMEM((own, parts, cells, channels), F32),
            pltpu.VMEM(w_qkv.shape, BF16),
            pltpu.VMEM(w_out.shape, BF16),
            block, block, block, block,
            pltpu.VMEM((n, channels), BF16),
            pltpu.VMEM((n, channels), BF16),
            pltpu.VMEM((n, 3 * channels), BF16),
            pltpu.VMEM((n, channels), BF16),
            pltpu.VMEM((n, channels), BF16),
            pltpu.VMEM((n, 3 * channels), BF16),
            pltpu.VMEM((HEADS * agents, channels), BF16),
            block,
            pltpu.VMEM((parts, own, cells, channels), BF16),
            pltpu.VMEM((2, 4, chips, 2 * share, channels), BF16),
            pltpu.VMEM((parts + 2 * MAXOFF, own, cells, channels), BF16),
            pieces, pieces,
            pltpu.VMEM((parts, chips, 2 * share, channels), BF16),
            line, line,
            pltpu.VMEM((2 * share, channels), BF16),
            pltpu.VMEM((parts, 2 * share, channels), BF16),
            pltpu.VMEM((8, 128), F32),
            pltpu.VMEM((tiles, 8, 128), F32),
            pltpu.SemaphoreType.DMA((4,)),
            dma(2), dma(parts), dma(parts), dma(parts), dma(2), dma(1), dma(parts), dma(chips), dma(parts), dma(tiles),
        ],
        compiler_params=pltpu.CompilerParams(
            collective_id=0, has_side_effects=True, vmem_limit_bytes=63 * 2**20
        ),
    )(feats.reshape(own, local, channels), types, valid, offsets, w_qkv, w_out, d_out)
    return (d_feats.reshape(feats.shape), g_qkv, g_out)


def solution(mesh):
    placed = (
        P("agent", "tile", None, None),
        P(),
        P(),
        P(),
        P(),
        P(),
        P("agent", "tile", None, None),
    )
    return jax.shard_map(
        body,
        mesh=mesh,
        in_specs=placed,
        out_specs=(P("agent", "tile", None, None), P(None, "tile", None), P(None, "tile", None)),
        check_vma=False,
    )
```
